256 devices in a mesh: hid: 64 (over x_hi, z, y), dp: 4 (over x_lo, core).
Axes of the slice: x: 4 (x_hi: 2, x_lo: 2; x = x_hi * 2 + x_lo), y: 4, z: 8, core: 2. Of those that a mesh axis runs over, the one named last changes fastest.
Arguments:
- tokens: bfloat16 [640, 7168], P('dp', 'hid'), may hold values from -6 to 6
- targets: bfloat16 [640, 7168], P('hid', 'dp'), may hold values from -6 to 6
- exp_gate: bfloat16 [7168, 32768], P('dp', 'hid'), may hold values from -0.0625 to 0.0625
- exp_up: bfloat16 [7168, 32768], P('dp', 'hid'), may hold values from -0.0625 to 0.0625
- exp_down: bfloat16 [32768, 7168], P('hid', 'dp'), may hold values from -6 to 6
- kept_block: int32 [64, 3], P('hid'), may hold values from 0 to 3, as said below
- dest_slot: int32 [64, 3], replicated, may hold values from 0 to 128, as said below
Outputs:
- gram_sum: float32 [16384, 16384], P('hid', 'dp')
- cross_prod: float32 [16384, 7168], P('hid', 'dp')
- dense_down: bfloat16 [16384, 7168], P('hid', 'dp')
The draws below stay inside these ranges and needn't reach their ends.
Inputs may be any that keep to these rules, and one draw needn't show every extreme that they name: `kept_block`: the entries of a row are distinct. `dest_slot`: each of 0 .. 127 stands exactly once; the value 128 marks a slot that keeps nothing; some row uses all 3 slots.
All inputs are finite; a program needn't handle non-finite values.
Results may differ from the reference program's by a relative error of at most 0.028.
Values may be sent and summed in bfloat16 or wider, within the bound.
No kernel may reach another device: no remote copies, remote signals or barrier semaphores. Data moves between devices by JAX's collectives and lax.ppermute only.
A program may use at most 128 MiB of HBM per device.

```python
import math
import jax
import jax.numpy as jnp
from jax import lax

D = 7168
BLK = 128
EBLK = 8
KEEP_DEV = 2
KEEP_MAX = 3
ROWS_DEV = 160
EXPERTS = 32
POOL = 32768
NB = 128
FF = 16384
TOKENS = 640
N_DP = 4


def draw_kept_block(key, part):
    key = jax.random.fold_in(key, 11)
    half_blocks = EBLK // 2
    scores = jax.random.randint(key, (2 * EXPERTS, half_blocks), 0, 2 ** 16) * half_blocks
    scores = scores + jnp.arange(half_blocks, dtype=jnp.int32)[None, :]
    ordering = jnp.argsort(scores, axis=1)
    return ordering[:, :KEEP_MAX].astype(jnp.int32)


def draw_dest_slot(key, part):
    key = jax.random.fold_in(key, 23)
    row_total = 2 * EXPERTS
    slot_total = row_total * KEEP_MAX
    key_favor, key_score = jax.random.split(key)
    favored = jax.random.randint(key_favor, (), 0, row_total)
    slot_row = jnp.arange(slot_total, dtype=jnp.int32) // KEEP_MAX
    scores = jax.random.randint(key_score, (slot_total,), 0, 2 ** 16) * slot_total
    scores = scores + jnp.arange(slot_total, dtype=jnp.int32)
    scores = scores - jnp.where(slot_row == favored, 2 ** 30, 0).astype(jnp.int32)
    ranking = jnp.argsort(jnp.argsort(scores)).astype(jnp.int32)
    block_total = KEEP_DEV * row_total
    dest = jnp.where(ranking < block_total, ranking, block_total)
    return dest.reshape(row_total, KEEP_MAX).astype(jnp.int32)


def level_of(rng, extent, cuts, low, largest):
    gain = 1.0
    for axis_at, shards_of in cuts:
        steps = jax.random.uniform(jax.random.fold_in(jax.random.fold_in(rng, 6), axis_at), (shards_of,), jnp.float32, low / len(cuts), largest / len(cuts))
        gain = gain * jnp.repeat(jnp.exp(steps), extent[axis_at] // shards_of).reshape((-1,) + (1,) * (len(extent) - 1 - axis_at))
    return gain


def scatter_about(key, dims, deviation, limit, shards=(), held_as=jnp.bfloat16):
    drawn = jax.random.normal(key, dims, jnp.float32) * deviation
    if len(shards) > 0:
        drawn = level_of(key, dims, shards, -0.22, 0.18) * drawn
    return jnp.clip(drawn, min=-limit, max=limit).astype(held_as)


def setup_inputs(seed: int = 0) -> dict:
    streams_of = jax.random.split(jax.random.key(seed), 8)
    tokens = scatter_about(streams_of[0], (TOKENS, D), 1.0, 6.0, ((0, 4), (1, 64)))
    targets = scatter_about(streams_of[1], (TOKENS, D), 1.0, 6.0, ((0, 64), (1, 4)))
    exp_gate = scatter_about(streams_of[2], (D, POOL), D ** -0.5, 0.0625, ((0, 4), (1, 64)))
    exp_up = scatter_about(streams_of[3], (D, POOL), D ** -0.5, 0.0625, ((0, 4), (1, 64)))
    exp_down = scatter_about(streams_of[4], (POOL, D), 1.0, 6.0, ((0, 64), (1, 4)))
    kept_block = draw_kept_block(jax.random.fold_in(streams_of[7], 71), 0)
    dest_slot = draw_dest_slot(jax.random.fold_in(streams_of[7], 71), 0)
    return dict(tokens=tokens, targets=targets, exp_gate=exp_gate, exp_up=exp_up, exp_down=exp_down, kept_block=kept_block, dest_slot=dest_slot)


def pool_columns(kept_block, dest_slot):
    slot_ids = jnp.arange(2 * EXPERTS * KEEP_MAX, dtype=jnp.int32)
    matches = dest_slot.reshape(-1)[None, :] == jnp.arange(NB, dtype=jnp.int32)[:, None]
    source = lax.optimization_barrier(jnp.sum(jnp.where(matches, slot_ids[None, :], 0), axis=1)).astype(jnp.int32)
    owner_half = (source // KEEP_MAX).astype(jnp.int32)
    block_ids = kept_block.reshape(-1)[source].astype(jnp.int32)
    first_unit = (owner_half * (EBLK // 2) + block_ids) * BLK
    return (first_unit[:, None] + jnp.arange(BLK, dtype=jnp.int32)[None, :]).reshape(-1)

def reference(tokens, targets, exp_gate, exp_up, exp_down, kept_block, dest_slot):
    columns = pool_columns(kept_block, dest_slot)
    dense_gate = exp_gate[:, columns]
    dense_up = exp_up[:, columns]
    dense_down = exp_down[columns, :]
    gate_sum = jnp.dot(tokens, dense_gate, preferred_element_type=jnp.float32)
    up_sum = jnp.dot(tokens, dense_up, preferred_element_type=jnp.float32)
    hidden = (jax.nn.silu(gate_sum) * up_sum).astype(jnp.bfloat16)
    scaling = 1.0 / math.sqrt(TOKENS)
    gram_sum = jnp.zeros((FF, FF), jnp.float32)
    for row_group in range(N_DP):
        block_rows = hidden[row_group * ROWS_DEV:(row_group + 1) * ROWS_DEV]
        partial_gram = jnp.dot(block_rows.T, block_rows, preferred_element_type=jnp.float32) * scaling
        rounded = lax.optimization_barrier(partial_gram.astype(jnp.bfloat16))
        gram_sum = gram_sum + rounded.astype(jnp.float32)
    cross_prod = jnp.dot(hidden.T, targets, preferred_element_type=jnp.float32) * scaling
    return (gram_sum, cross_prod, dense_down)
```

```python
import math

import jax
import jax.numpy as jnp
from jax import lax
from jax.experimental import pallas as pl
from jax.experimental.pallas import tpu as pltpu
from jax.sharding import Mesh
from jax.sharding import PartitionSpec as P

BLK = 128
SUB = 32
SLOTS = 3
XH, NZ, NY, XL, NC = 2, 8, 4, 2, 2
HID = ("xh", "z", "y")
DP = ("xl", "c")
N_HID = XH * NZ * NY
N_DP = XL * NC
N_XZ = XH * NZ
A_COLS = 640
BF16 = jnp.bfloat16
F32 = jnp.float32
VMEM = pl.BlockSpec(memory_space=pltpu.VMEM)
ANY = pl.BlockSpec(memory_space=pl.ANY)
SMEM = pl.BlockSpec(memory_space=pltpu.SMEM)
PARAMS = pltpu.CompilerParams(vmem_limit_bytes=56 * 1024 * 1024)


def call(kernel, out_shape, in_specs, scratch, *args):
    outs = jax.tree.map(lambda _: VMEM, out_shape)
    return pl.pallas_call(
        kernel,
        out_shape=out_shape,
        in_specs=in_specs,
        out_specs=outs,
        scratch_shapes=scratch,
        compiler_params=PARAMS,
    )(*args)


def struct(shape, dtype):
    return jax.ShapeDtypeStruct(shape, dtype)


def project_kernel(where, kept, here, low, high, far0, far1, gate, up, out0, out1, out2, out3, lhs, rhs):
    outs = (out0, out1, out2, out3)
    y, me = where[0], where[1]
    rows, lanes = here.shape[1], here.shape[2]
    width = gate.shape[0] // (N_HID // N_DP)
    per = N_XZ // N_DP
    half = far0.shape[0]
    for k in range(NY):
        for d in range(N_DP):
            for zl in range(per):
                at = d * per + zl
                if k < 3:
                    piece = (here, low, high)[k][at]
                else:
                    piece = far0[at] if at < half else far1[at - half]
                col = (k * per + zl) * lanes
                lhs[d * rows : (d + 1) * rows, col : col + lanes] = piece
    for slot in range(SLOTS):
        start = pl.multiple_of(kept[0, slot] * BLK, BLK)
        for side, weight in enumerate((gate, up)):
            col = (2 * slot + side) * BLK
            for k in range(NY):
                other = lax.rem(y + (0, 3, 1, 2)[k], NY)
                for zl in range(per):
                    at = (k * per + zl) * lanes
                    first = pl.multiple_of((zl * NY + other) * width, 16)
                    rhs[at : at + width, col : col + BLK] = weight[pl.ds(first, width), pl.ds(start, BLK)]
                    rhs[at + width : at + lanes, col : col + BLK] = jnp.zeros((lanes - width, BLK), BF16)
        for k in range(N_DP):
            first = pl.multiple_of((me ^ k) * rows, 16)
            outs[k][:, 2 * slot * BLK : (2 * slot + 2) * BLK] = jnp.dot(
                lhs[pl.ds(first, rows), :],
                rhs[:, 2 * slot * BLK : (2 * slot + 2) * BLK],
                preferred_element_type=F32,
            ).astype(BF16)


def lane_group(shape):
    return lax.broadcasted_iota(jnp.int32, shape, len(shape) - 1) // SUB


def activate_kernel(part0, part1, part2, part3, after, out, wide):
    rows = part0.shape[0]
    step = rows // N_XZ
    hidden = []
    for slot in range(SLOTS):
        total = part0[:, 2 * slot * BLK : (2 * slot + 2) * BLK].astype(F32)
        for part in (part1, part2, part3):
            total = total + part[:, 2 * slot * BLK : (2 * slot + 2) * BLK].astype(F32)
        gate, up = total[:, :BLK], total[:, BLK:]
        hidden.append(gate / (1.0 + jnp.exp(-gate)) * up)
    group = lane_group((rows, BLK))
    wide[rows:, :] = jnp.zeros((16, BLK), F32)
    for y in range(NY):
        mixed = jnp.zeros((rows, BLK), F32)
        for slot in range(SLOTS):
            shift = (slot - y) % NY * SUB
            rolled = pltpu.roll(hidden[slot], shift, 1) if shift else hidden[slot]
            mixed = jnp.where(group == slot, rolled, mixed)
        wide[:rows, :] = mixed
        for xz in range(N_XZ):
            out[xz * NY + y] = wide[step * xz : step * xz + 16, :].astype(BF16)


def arrange_kernel(where, source, got, after, out0, out1, out2, out3, send_own, quarters):
    me = where[1]
    group = lane_group((16, BLK))
    per_quarter = source.shape[0] // NY // N_DP
    for t in range(source.shape[0] // NY):
        mixed = jnp.zeros((16, BLK), F32)
        for b in range(NY):
            slot_id = source[t * NY + b]
            row = slot_id // SLOTS
            slot = slot_id - row * SLOTS
            shift = lax.rem((b - slot + NY) * SUB, BLK)
            rolled = pltpu.roll(got[row].astype(F32), shift, 1)
            mixed = jnp.where(group == b, rolled, mixed)
        mixed = mixed.astype(BF16)
        at = t % per_quarter * BLK
        quarters[t // per_quarter, :, at : at + BLK] = mixed
        send_own[2 * t] = mixed
        send_own[2 * t + 1] = mixed
    for k, out in enumerate((out0, out1, out2, out3)):
        out[...] = quarters[me ^ k]


def own_kernel(odd, got, out, wide):
    group = lane_group((16, BLK))
    step = out.shape[0] // N_XZ
    back = odd[0] * (2 * SUB)
    for xz in range(N_XZ):
        pieces = [got[xz * NY + y].astype(F32) for y in range(NY)]
        for blk in range(2):
            mixed = jnp.zeros((16, BLK), F32)
            for y in range(NY):
                shift = lax.rem(2 * BLK + (y - blk) * SUB - back, BLK)
                mixed = jnp.where(group == y, pltpu.roll(pieces[y], shift, 1), mixed)
            wide[xz * step : xz * step + 16, blk * BLK : (blk + 1) * BLK] = mixed
    out[...] = wide[: out.shape[0], :].astype(BF16)


def turn_kernel(own0, own1, own2, own3, out, parts, wide):
    step = own0.shape[0] // N_XZ
    for k, own in enumerate((own0, own1, own2, own3)):
        parts[k, : own.shape[0], :] = own[...].astype(F32)
        parts[k, own.shape[0] :, :] = jnp.zeros((16, own.shape[1]), F32)
    for xz in range(N_XZ):
        for k in range(N_DP):
            at = (xz * N_DP + k) * step
            wide[at : at + 16, :] = parts[k, xz * step : xz * step + 16, :]
    out[...] = wide[: out.shape[1], :].T.astype(BF16)


def cross_kernel(scaling, where, own0, own1, own2, own3, targets, out):
    rows = own0.shape[0]
    total = jnp.zeros(out.shape, F32)
    for k, own in enumerate((own0, own1, own2, own3)):
        first = pl.multiple_of((where[1] ^ k) * rows, 16)
        total += lax.dot_general(
            own[...], targets[pl.ds(first, rows), :], (((0,), (0,)), ((), ())), preferred_element_type=F32
        )
    out[...] = total * scaling


def gram_kernel(scaling, where, own, a_here, a_low, a_high, a_far0, a_far1, b_all, out, acc):
    y = where[0]
    half = a_far0.shape[0]

    def put(at, value):
        acc[at, :, :A_COLS] = value

    put(y, jnp.dot(own[...], a_here[...], preferred_element_type=F32))
    put(lax.rem(y + 3, NY), jnp.dot(own[...], a_low[...], preferred_element_type=F32))
    put(lax.rem(y + 1, NY), jnp.dot(own[...], a_high[...], preferred_element_type=F32))
    put(
        lax.rem(y + 2, NY),
        jnp.dot(own[:, :half], a_far0[...], preferred_element_type=F32)
        + jnp.dot(own[:, half:], a_far1[...], preferred_element_type=F32),
    )
    for at in range(NY):
        acc[at, :, A_COLS:] = jnp.dot(own[...], b_all[at], preferred_element_type=F32)
    group = lane_group((out.shape[0], BLK))
    for t in range(out.shape[1] // BLK // NY):
        parts = [acc[at, :, t * BLK : (t + 1) * BLK] * scaling for at in range(NY)]
        for b in range(NY):
            mixed = parts[b]
            for at in range(NY):
                if at != b:
                    mixed = jnp.where(group == at, pltpu.roll(parts[at], (at - b) % NY * SUB, 1), mixed)
            col = (t * NY + b) * BLK
            out[:, col : col + BLK] = mixed


def after_kernel(values, after, out):
    for i in range(values.shape[0]):
        for j in range(values.shape[1]):
            out[i, j] = values[i, j]


def copy_kernel(x, after, out):
    out[...] = x[...]


def after(values, *others):
    return pl.pallas_call(
        lambda got, *rest: after_kernel(got, rest[:-1], rest[-1]),
        out_shape=struct(values.shape, values.dtype),
        in_specs=[SMEM] + [ANY] * len(others),
        out_specs=SMEM,
    )(values, *others)


def pick_sources(dest_slot, block_count):
    slot_total = dest_slot.shape[0] * dest_slot.shape[1]
    slot_ids = jnp.arange(slot_total, dtype=jnp.int32)
    matches = dest_slot.reshape(-1)[None, :] == jnp.arange(block_count, dtype=jnp.int32)[:, None]
    return jnp.sum(jnp.where(matches, slot_ids[None, :], 0), axis=1)


def exchange(values):
    got = [values[0]]
    for k in range(1, N_DP):
        got.append(lax.ppermute(values[k], DP, [(i, i ^ k) for i in range(N_DP)]))
    return got


def swap_pairs():
    pairs = []
    for xh in range(2):
        for zh in range(2):
            for rest in range(16):
                for xl in range(2):
                    for c in range(2):
                        here = ((xh * 2 + zh) * 16 + rest) * 4 + xl * 2 + c
                        there = ((xl * 2 + c) * 16 + rest) * 4 + xh * 2 + zh
                        pairs.append((here, there))
    return pairs


def shift(x, axis, size, step):
    return lax.ppermute(x, axis, [(i, (i + step) % size) for i in range(size)])


def gather_copies(x, axis, size):
    copies = jnp.broadcast_to(x[None], (size, *x.shape))
    return lax.all_to_all(copies, axis, split_axis=0, concat_axis=0, tiled=True)


def ring(x, axis, size):
    found, low, high = [], x, x
    for step in range(1, size // 2):
        low, high = shift(low, axis, size, 1), shift(high, axis, size, -1)
        found += [(-step, low), (step, high)]
    half = x.shape[0] // 2
    far0 = shift(low[:half], axis, size, 1)
    far1 = shift(high[half:], axis, size, -1)
    return found, far0, far1


def local(tokens, targets, exp_gate, exp_up, exp_down, kept_block, dest_slot):
    rows = tokens.shape[0]
    quarter = exp_gate.shape[0]
    local_width = exp_gate.shape[1] // 2
    scaling = 1.0 / math.sqrt(rows * N_DP)
    xh, z, y = (lax.axis_index(name) for name in HID)
    where = jnp.stack([y, lax.axis_index(DP)]).astype(jnp.int32)
    source = pick_sources(dest_slot, 2 * N_HID)

    def both_halves(x):
        other = shift(x, "xh", XH, 1)
        return jnp.where(xh == 0, jnp.stack([x, other]), jnp.stack([other, x]))

    moved = lax.ppermute(tokens, HID + DP, swap_pairs())
    moved = jnp.pad(moved, ((0, 0), (0, BLK - moved.shape[1])))
    here = gather_copies(moved, ("xh", "z"), N_XZ)
    ((_, low), (_, high)), far0, far1 = ring(here, "y", NY)

    all_targets = both_halves(lax.all_gather(targets, "y", axis=0, tiled=True))
    all_targets = lax.all_gather(all_targets, "z", axis=0, tiled=False)
    all_targets = all_targets.transpose(1, 0, 2, 3).reshape(N_DP * rows, -1)

    chosen = after(kept_block, here)[0]
    down = exp_down.reshape(-1, N_HID, BLK // N_HID, quarter)[chosen]
    down = lax.all_to_all(down, HID, split_axis=1, concat_axis=0, tiled=True)

    parts = call(
        project_kernel,
        (struct((rows, 2 * SLOTS * BLK), BF16),) * N_DP,
        [SMEM, SMEM] + [VMEM] * 7,
        [pltpu.VMEM((N_DP * rows, 16 * BLK), BF16), pltpu.VMEM((16 * BLK, 2 * SLOTS * BLK), BF16)],
        where,
        kept_block,
        here,
        low,
        high,
        far0,
        far1,
        exp_gate,
        exp_up,
    )
    spread = call(
        activate_kernel,
        struct((N_HID, 16, BLK), BF16),
        [VMEM] * N_DP + [ANY],
        [pltpu.VMEM((rows + 16, BLK), F32)],
        *exchange(parts),
        down,
    )
    spread = lax.all_to_all(spread, HID, split_axis=0, concat_axis=0, tiled=True)
    *quarters, send_own = call(
        arrange_kernel,
        (struct((16, 1024), BF16),) * N_DP + (struct((N_HID, 16, BLK), BF16),),
        [SMEM, SMEM, VMEM, ANY],
        [pltpu.VMEM((N_DP, 16, 1024), BF16)],
        where,
        source,
        spread,
        all_targets,
    )
    step = rows // N_XZ
    mine = jnp.concatenate([x[:step] for x in exchange(quarters)], axis=0)

    a_here = gather_copies(mine[:, :A_COLS], ("xh", "z"), N_XZ).reshape(N_DP * rows, A_COLS)
    ((_, a_low), (_, a_high)), a_far0, a_far1 = ring(a_here, "y", NY)

    b_block = both_halves(mine[:, A_COLS:])
    b_wide = jnp.zeros((NY, *b_block.shape), BF16)

    def put_y(whole, at, value, first=0):
        return lax.dynamic_update_slice(whole, value[None], (at % NY, first, 0, 0))

    b_wide = put_y(b_wide, y, b_block)
    found, far0, far1 = ring(b_block, "y", NY)
    for offset, value in found:
        b_wide = put_y(b_wide, y + offset + NY, value)
    b_wide = put_y(b_wide, y + NY // 2, far0)
    b_wide = put_y(b_wide, y + NY // 2, far1, 1)
    b_all = jnp.zeros((NY, XH, NZ, *b_wide.shape[2:]), BF16)

    def put_z(whole, at, value, first=0):
        return lax.dynamic_update_slice(whole, value[:, :, None], (first, 0, at % NZ, 0, 0))

    b_all = put_z(b_all, z, b_wide)
    found, far0, far1 = ring(b_wide, "z", NZ)
    for offset, value in found:
        b_all = put_z(b_all, z + offset + NZ, value)
    b_all = put_z(b_all, z + NZ // 2, far0)
    b_all = put_z(b_all, z + NZ // 2, far1, 2)
    b_all = b_all.reshape(NY, N_DP * rows, -1)

    send_own = call(copy_kernel, struct(send_own.shape, BF16), [VMEM, ANY], [], send_own, a_here)
    got_own = lax.all_to_all(send_own, HID, split_axis=0, concat_axis=0, tiled=True)
    own = call(
        own_kernel,
        struct((rows, local_width), BF16),
        [SMEM, VMEM],
        [pltpu.VMEM((rows + 16, local_width), F32)],
        lax.rem(y, 2).reshape(1),
        got_own,
    )
    own = exchange([own] * N_DP)
    own_turned = call(
        turn_kernel,
        struct((local_width, N_DP * rows), BF16),
        [VMEM] * N_DP,
        [pltpu.VMEM((N_DP, rows + 16, local_width), F32), pltpu.VMEM((N_DP * rows + 16, local_width), F32)],
        *own,
    )
    cross_prod = call(
        lambda *refs: cross_kernel(scaling, *refs),
        struct((local_width, quarter), F32),
        [SMEM] + [VMEM] * 5,
        [],
        where,
        *own,
        all_targets,
    )
    gram_sum = call(
        lambda *refs: gram_kernel(scaling, *refs),
        struct((local_width, N_HID // N_DP * local_width), F32),
        [SMEM] + [VMEM] * 7,
        [pltpu.VMEM((NY, local_width, 1024), F32)],
        where,
        own_turned,
        a_here,
        a_low,
        a_high,
        a_far0,
        a_far1,
        b_all,
    )

    picked = after(source[None], got_own)[0]
    down = jnp.take(down.reshape(N_HID * SLOTS, BLK // N_HID, quarter), picked, axis=0)
    down = down.reshape(N_HID, 2, BLK // N_HID, quarter)
    down = lax.all_to_all(down, HID, split_axis=0, concat_axis=0, tiled=True)
    dense_down = down.transpose(1, 0, 2, 3).reshape(local_width, quarter)
    return (gram_sum, cross_prod, dense_down)


def solution(mesh):
    fine = Mesh(mesh.devices.reshape(XH, NZ, NY, XL, NC), HID + DP)
    return jax.shard_map(
        local,
        mesh=fine,
        in_specs=(P(DP, HID), P(HID, DP), P(DP, HID), P(DP, HID), P(HID, DP), P(HID, None), P()),
        out_specs=(P(HID, DP), P(HID, DP), P(HID, DP)),
        check_vma=False,
    )
```

```python
import math

import jax
import jax.numpy as jnp
from jax import lax
from jax.experimental import pallas as pl
from jax.experimental.pallas import tpu as pltpu
from jax.sharding import Mesh
from jax.sharding import PartitionSpec as P

BLK = 128
SUB = 32
SLOTS = 3
XH, NZ, NY, XL, NC = 2, 8, 4, 2, 2
HID = ("xh", "z", "y")
DP = ("xl", "c")
N_HID = XH * NZ * NY
N_DP = XL * NC
N_XZ = XH * NZ
A_COLS = 640
BF16 = jnp.bfloat16
F32 = jnp.float32
VMEM = pl.BlockSpec(memory_space=pltpu.VMEM)
ANY = pl.BlockSpec(memory_space=pl.ANY)
SMEM = pl.BlockSpec(memory_space=pltpu.SMEM)
PARAMS = pltpu.CompilerParams(vmem_limit_bytes=56 * 1024 * 1024)


def call(kernel, out_shape, in_specs, scratch, *args):
    outs = jax.tree.map(lambda _: VMEM, out_shape)
    return pl.pallas_call(
        kernel,
        out_shape=out_shape,
        in_specs=in_specs,
        out_specs=outs,
        scratch_shapes=scratch,
        compiler_params=PARAMS,
    )(*args)


def struct(shape, dtype):
    return jax.ShapeDtypeStruct(shape, dtype)


def project_kernel(where, kept, here, low, high, far, gate, up, out0, out1, out2, out3, lhs, rhs):
    outs = (out0, out1, out2, out3)
    y, me = where[0], where[1]
    rows, lanes = here.shape[1], here.shape[2]
    width = gate.shape[0] // (N_HID // N_DP)
    per = N_XZ // N_DP
    for k in range(NY):
        for d in range(N_DP):
            for zl in range(per):
                at = d * per + zl
                col = (k * per + zl) * lanes
                lhs[d * rows : (d + 1) * rows, col : col + lanes] = (here, low, high, far)[k][at]
    for slot in range(SLOTS):
        start = pl.multiple_of(kept[0, slot] * BLK, BLK)
        for side, weight in enumerate((gate, up)):
            col = (2 * slot + side) * BLK
            for k in range(NY):
                other = lax.rem(y + (0, 3, 1, 2)[k], NY)
                for zl in range(per):
                    at = (k * per + zl) * lanes
                    first = pl.multiple_of((zl * NY + other) * width, 16)
                    rhs[at : at + width, col : col + BLK] = weight[pl.ds(first, width), pl.ds(start, BLK)]
                    rhs[at + width : at + lanes, col : col + BLK] = jnp.zeros((lanes - width, BLK), BF16)
        for k in range(N_DP):
            first = pl.multiple_of((me ^ k) * rows, 16)
            outs[k][:, 2 * slot * BLK : (2 * slot + 2) * BLK] = jnp.dot(
                lhs[pl.ds(first, rows), :],
                rhs[:, 2 * slot * BLK : (2 * slot + 2) * BLK],
                preferred_element_type=F32,
            ).astype(BF16)


def lane_group(shape):
    return lax.broadcasted_iota(jnp.int32, shape, len(shape) - 1) // SUB


def activate_kernel(part0, part1, part2, part3, after, out, wide):
    rows = part0.shape[0]
    step = rows // N_XZ
    hidden = []
    for slot in range(SLOTS):
        total = part0[:, 2 * slot * BLK : (2 * slot + 2) * BLK].astype(F32)
        for part in (part1, part2, part3):
            total = total + part[:, 2 * slot * BLK : (2 * slot + 2) * BLK].astype(F32)
        gate, up = total[:, :BLK], total[:, BLK:]
        hidden.append(gate / (1.0 + jnp.exp(-gate)) * up)
    group = lane_group((rows, BLK))
    wide[rows:, :] = jnp.zeros((16, BLK), F32)
    for y in range(NY):
        mixed = jnp.zeros((rows, BLK), F32)
        for slot in range(SLOTS):
            shift = (slot - y) % NY * SUB
            rolled = pltpu.roll(hidden[slot], shift, 1) if shift else hidden[slot]
            mixed = jnp.where(group == slot, rolled, mixed)
        wide[:rows, :] = mixed
        for xz in range(N_XZ):
            out[xz * NY + y] = wide[step * xz : step * xz + 16, :].astype(BF16)


def arrange_kernel(where, source, got, after0, after1, out0, out1, out2, out3, send_own, quarters):
    me = where[1]
    group = lane_group((16, BLK))
    per_quarter = source.shape[0] // NY // N_DP
    for t in range(source.shape[0] // NY):
        mixed = jnp.zeros((16, BLK), F32)
        for b in range(NY):
            slot_id = source[t * NY + b]
            row = slot_id // SLOTS
            slot = slot_id - row * SLOTS
            shift = lax.rem((b - slot + NY) * SUB, BLK)
            rolled = pltpu.roll(got[row].astype(F32), shift, 1)
            mixed = jnp.where(group == b, rolled, mixed)
        mixed = mixed.astype(BF16)
        at = t % per_quarter * BLK
        quarters[t // per_quarter, :, at : at + BLK] = mixed
        send_own[2 * t] = mixed
        send_own[2 * t + 1] = mixed
    for k, out in enumerate((out0, out1, out2, out3)):
        out[...] = quarters[me ^ k]


def own_kernel(odd, got, *refs):
    out, wide = refs[-2:]
    group = lane_group((16, BLK))
    step = out.shape[0] // N_XZ
    back = odd[0] * (2 * SUB)
    for xz in range(N_XZ):
        pieces = [got[xz * NY + y].astype(F32) for y in range(NY)]
        for blk in range(2):
            mixed = jnp.zeros((16, BLK), F32)
            for y in range(NY):
                shift = lax.rem(2 * BLK + (y - blk) * SUB - back, BLK)
                mixed = jnp.where(group == y, pltpu.roll(pieces[y], shift, 1), mixed)
            wide[xz * step : xz * step + 16, blk * BLK : (blk + 1) * BLK] = mixed
    out[...] = wide[: out.shape[0], :].astype(BF16)


def turn_kernel(own0, own1, own2, own3, *refs):
    out, parts, wide = refs[-3:]
    step = own0.shape[0] // N_XZ
    for k, own in enumerate((own0, own1, own2, own3)):
        parts[k, : own.shape[0], :] = own[...].astype(F32)
        parts[k, own.shape[0] :, :] = jnp.zeros((16, own.shape[1]), F32)
    for xz in range(N_XZ):
        for k in range(N_DP):
            at = (xz * N_DP + k) * step
            wide[at : at + 16, :] = parts[k, xz * step : xz * step + 16, :]
    out[...] = wide[: out.shape[1], :].T.astype(BF16)


def cross_kernel(scaling, where, own0, own1, own2, own3, targets, out):
    rows = own0.shape[0]
    total = jnp.zeros(out.shape, F32)
    for k, own in enumerate((own0, own1, own2, own3)):
        first = pl.multiple_of((where[1] ^ k) * rows, 16)
        total += lax.dot_general(
            own[...], targets[pl.ds(first, rows), :], (((0,), (0,)), ((), ())), preferred_element_type=F32
        )
    out[...] = total * scaling


def gram_kernel(scaling, where, own, a_here, a_low, a_high, a_far0, a_far1, b_all, out, acc):
    y = where[0]
    half = a_far0.shape[0]

    def put(at, value):
        acc[at, :, :A_COLS] = value

    put(y, jnp.dot(own[...], a_here[...], preferred_element_type=F32))
    put(lax.rem(y + 3, NY), jnp.dot(own[...], a_low[...], preferred_element_type=F32))
    put(lax.rem(y + 1, NY), jnp.dot(own[...], a_high[...], preferred_element_type=F32))
    put(
        lax.rem(y + 2, NY),
        jnp.dot(own[:, :half], a_far0[...], preferred_element_type=F32)
        + jnp.dot(own[:, half:], a_far1[...], preferred_element_type=F32),
    )
    for at in range(NY):
        acc[at, :, A_COLS:] = jnp.dot(own[...], b_all[at], preferred_element_type=F32)
    group = lane_group((out.shape[0], BLK))
    for t in range(out.shape[1] // BLK // NY):
        parts = [acc[at, :, t * BLK : (t + 1) * BLK] * scaling for at in range(NY)]
        for b in range(NY):
            mixed = parts[b]
            for at in range(NY):
                if at != b:
                    mixed = jnp.where(group == at, pltpu.roll(parts[at], (at - b) % NY * SUB, 1), mixed)
            col = (t * NY + b) * BLK
            out[:, col : col + BLK] = mixed


def after_kernel(values, after, out):
    for i in range(values.shape[0]):
        for j in range(values.shape[1]):
            out[i, j] = values[i, j]


def copy_kernel(x, *refs):
    refs[-1][...] = x[...]


def after(values, *others):
    return pl.pallas_call(
        lambda got, *rest: after_kernel(got, rest[:-1], rest[-1]),
        out_shape=struct(values.shape, values.dtype),
        in_specs=[SMEM] + [ANY] * len(others),
        out_specs=SMEM,
    )(values, *others)


def pick_sources(dest_slot, block_count):
    slot_total = dest_slot.shape[0] * dest_slot.shape[1]
    slot_ids = jnp.arange(slot_total, dtype=jnp.int32)
    matches = dest_slot.reshape(-1)[None, :] == jnp.arange(block_count, dtype=jnp.int32)[:, None]
    return jnp.sum(jnp.where(matches, slot_ids[None, :], 0), axis=1)


def exchange(values):
    got = [values[0]]
    for k in range(1, N_DP):
        got.append(lax.ppermute(values[k], DP, [(i, i ^ k) for i in range(N_DP)]))
    return got


def swap_pairs():
    pairs = []
    for xh in range(2):
        for zh in range(2):
            for rest in range(16):
                for xl in range(2):
                    for c in range(2):
                        here = ((xh * 2 + zh) * 16 + rest) * 4 + xl * 2 + c
                        there = ((xl * 2 + c) * 16 + rest) * 4 + xh * 2 + zh
                        pairs.append((here, there))
    return pairs


def shift(x, axis, size, step):
    return lax.ppermute(x, axis, [(i, (i + step) % size) for i in range(size)])


def gather_copies(x, axis, size):
    copies = jnp.broadcast_to(x[None], (size, *x.shape))
    return lax.all_to_all(copies, axis, split_axis=0, concat_axis=0, tiled=True)


def ring(x, axis, size):
    found, low, high = [], x, x
    for step in range(1, size // 2):
        low, high = shift(low, axis, size, 1), shift(high, axis, size, -1)
        found += [(-step, low), (step, high)]
    half = x.shape[0] // 2
    far0 = shift(low[:half], axis, size, 1)
    far1 = shift(high[half:], axis, size, -1)
    return found, far0, far1


def local(tokens, targets, exp_gate, exp_up, exp_down, kept_block, dest_slot):
    rows = tokens.shape[0]
    quarter = exp_gate.shape[0]
    local_width = exp_gate.shape[1] // 2
    scaling = 1.0 / math.sqrt(rows * N_DP)
    xh, z, y = (lax.axis_index(name) for name in HID)
    where = jnp.stack([y, lax.axis_index(DP)]).astype(jnp.int32)
    source = pick_sources(dest_slot, 2 * N_HID)

    def both_halves(x):
        other = shift(x, "xh", XH, 1)
        return jnp.where(xh == 0, jnp.stack([x, other]), jnp.stack([other, x]))

    moved = lax.ppermute(tokens, HID + DP, swap_pairs())
    moved = jnp.pad(moved, ((0, 0), (0, BLK - moved.shape[1])))
    here = gather_copies(moved, ("xh", "z"), N_XZ)
    low, high, far = (shift(here, "y", NY, step) for step in (1, -1, 2))

    all_targets = lax.all_gather(both_halves(targets), ("z", "y"), axis=0, tiled=False)
    all_targets = all_targets.transpose(1, 0, 2, 3).reshape(N_DP * rows, -1)

    chosen = after(kept_block, low)[0]
    down = exp_down.reshape(-1, N_HID, BLK // N_HID, quarter)[chosen]
    down = lax.all_to_all(down, HID, split_axis=1, concat_axis=0, tiled=True)

    parts = call(
        project_kernel,
        (struct((rows, 2 * SLOTS * BLK), BF16),) * N_DP,
        [SMEM, SMEM] + [VMEM] * 6,
        [pltpu.VMEM((N_DP * rows, 16 * BLK), BF16), pltpu.VMEM((16 * BLK, 2 * SLOTS * BLK), BF16)],
        where,
        kept_block,
        here,
        low,
        high,
        far,
        exp_gate,
        exp_up,
    )
    spread = call(
        activate_kernel,
        struct((N_HID, 16, BLK), BF16),
        [VMEM] * N_DP + [ANY],
        [pltpu.VMEM((rows + 16, BLK), F32)],
        *exchange(parts),
        down,
    )
    spread = lax.all_to_all(spread, HID, split_axis=0, concat_axis=0, tiled=True)
    down = down.reshape(N_HID * SLOTS, BLK // N_HID, quarter).at[source].get(mode="promise_in_bounds")
    *quarters, send_own = call(
        arrange_kernel,
        (struct((16, 1024), BF16),) * N_DP + (struct((N_HID, 16, BLK), BF16),),
        [SMEM, SMEM, VMEM, ANY, ANY],
        [pltpu.VMEM((N_DP, 16, 1024), BF16)],
        where,
        source,
        spread,
        all_targets,
        down,
    )
    step = rows // N_XZ
    mine = jnp.concatenate([x[:step] for x in exchange(quarters)], axis=0)

    a_here = gather_copies(mine[:, :A_COLS], ("xh", "z"), N_XZ).reshape(N_DP * rows, A_COLS)
    ((_, a_low), (_, a_high)), a_far0, a_far1 = ring(a_here, "y", NY)

    b_block = both_halves(mine[:, A_COLS:])
    b_wide = jnp.zeros((NY, *b_block.shape), BF16)

    def put_y(whole, at, value, first=0):
        return lax.dynamic_update_slice(whole, value[None], (at % NY, first, 0, 0))

    b_wide = put_y(b_wide, y, b_block)
    found, far0, far1 = ring(b_block, "y", NY)
    for offset, value in found:
        b_wide = put_y(b_wide, y + offset + NY, value)
    b_wide = put_y(b_wide, y + NY // 2, far0)
    b_wide = put_y(b_wide, y + NY // 2, far1, 1)
    b_all = jnp.zeros((NY, XH, NZ, *b_wide.shape[2:]), BF16)

    def put_z(whole, at, value, first=0):
        return lax.dynamic_update_slice(whole, value[:, :, None], (first, 0, at % NZ, 0, 0))

    b_all = put_z(b_all, z, b_wide)
    found, far0, far1 = ring(b_wide, "z", NZ)
    b_steps = [value for _, value in found]
    for offset, value in found:
        b_all = put_z(b_all, z + offset + NZ, value)
    b_all = put_z(b_all, z + NZ // 2, far0)
    b_all = put_z(b_all, z + NZ // 2, far1, 2)
    b_all = b_all.reshape(NY, N_DP * rows, -1)

    send_own = call(copy_kernel, struct(send_own.shape, BF16), [VMEM, ANY, ANY], [], send_own, a_here, b_wide)
    got_own = lax.all_to_all(send_own, HID, split_axis=0, concat_axis=0, tiled=True)
    own = call(
        own_kernel,
        struct((rows, local_width), BF16),
        [SMEM, VMEM] + [ANY] * 6,
        [pltpu.VMEM((rows + 16, local_width), F32)],
        lax.rem(y, 2).reshape(1),
        got_own,
        a_low,
        a_high,
        *b_steps[:4],
    )
    own = exchange([own] * N_DP)
    own_turned = call(
        turn_kernel,
        struct((local_width, N_DP * rows), BF16),
        [VMEM] * N_DP + [ANY] * 4,
        [pltpu.VMEM((N_DP, rows + 16, local_width), F32), pltpu.VMEM((N_DP * rows + 16, local_width), F32)],
        *own,
        a_far0,
        a_far1,
        *b_steps[4:],
    )
    cross_prod = call(
        lambda *refs: cross_kernel(scaling, *refs),
        struct((local_width, quarter), F32),
        [SMEM] + [VMEM] * 5,
        [],
        where,
        *own,
        all_targets,
    )
    gram_sum = call(
        lambda *refs: gram_kernel(scaling, *refs),
        struct((local_width, N_HID // N_DP * local_width), F32),
        [SMEM] + [VMEM] * 7,
        [pltpu.VMEM((NY, local_width, 1024), F32)],
        where,
        own_turned,
        a_here,
        a_low,
        a_high,
        a_far0,
        a_far1,
        b_all,
    )

    down = call(copy_kernel, struct(down.shape, BF16), [VMEM, ANY], [], down, got_own)
    down = lax.all_to_all(down.reshape(N_HID, 2, BLK // N_HID, quarter), HID, split_axis=0, concat_axis=0, tiled=True)
    dense_down = down.transpose(1, 0, 2, 3).reshape(local_width, quarter)
    return (gram_sum, cross_prod, dense_down)


def solution(mesh):
    fine = Mesh(mesh.devices.reshape(XH, NZ, NY, XL, NC), HID + DP)
    return jax.shard_map(
        local,
        mesh=fine,
        in_specs=(P(DP, HID), P(HID, DP), P(DP, HID), P(DP, HID), P(HID, DP), P(HID, None), P()),
        out_specs=(P(HID, DP), P(HID, DP), P(HID, DP)),
        check_vma=False,
    )
```

```python
import math

import jax
import jax.numpy as jnp
from jax import lax
from jax.experimental import pallas as pl
from jax.experimental.pallas import tpu as pltpu
from jax.sharding import Mesh
from jax.sharding import PartitionSpec as P

BLK = 128
SUB = 32
SLOTS = 3
XH, NZ, NY, XL, NC = 2, 8, 4, 2, 2
HID = ("xh", "z", "y")
DP = ("xl", "c")
N_HID = XH * NZ * NY
N_DP = XL * NC
N_XZ = XH * NZ
BF16 = jnp.bfloat16
F32 = jnp.float32
VMEM = pl.BlockSpec(memory_space=pltpu.VMEM)
ANY = pl.BlockSpec(memory_space=pl.ANY)
SMEM = pl.BlockSpec(memory_space=pltpu.SMEM)
PARAMS = pltpu.CompilerParams(vmem_limit_bytes=56 * 1024 * 1024)


def call(kernel, out_shape, in_specs, scratch, *args):
    outs = jax.tree.map(lambda _: VMEM, out_shape)
    return pl.pallas_call(
        kernel,
        out_shape=out_shape,
        in_specs=in_specs,
        out_specs=outs,
        scratch_shapes=scratch,
        compiler_params=PARAMS,
    )(*args)


def struct(shape, dtype):
    return jax.ShapeDtypeStruct(shape, dtype)


def project_kernel(where, kept, here, low, high, far0, far1, gate, up, out0, out1, out2, out3, lhs, rhs):
    outs = (out0, out1, out2, out3)
    y, me = where[0], where[1]
    rows, lanes = here.shape[1], here.shape[2]
    width = gate.shape[0] // (N_HID // N_DP)
    per = N_XZ // N_DP
    half = far0.shape[0]
    for k in range(NY):
        for d in range(N_DP):
            for zl in range(per):
                at = d * per + zl
                if k < 3:
                    piece = (here, low, high)[k][at]
                else:
                    piece = far0[at] if at < half else far1[at - half]
                col = (k * per + zl) * lanes
                lhs[d * rows : (d + 1) * rows, col : col + lanes] = piece
    for slot in range(SLOTS):
        start = pl.multiple_of(kept[0, slot] * BLK, BLK)
        for side, weight in enumerate((gate, up)):
            col = (2 * slot + side) * BLK
            for k in range(NY):
                other = lax.rem(y + (0, 3, 1, 2)[k], NY)
                for zl in range(per):
                    at = (k * per + zl) * lanes
                    first = pl.multiple_of((zl * NY + other) * width, 16)
                    rhs[at : at + width, col : col + BLK] = weight[pl.ds(first, width), pl.ds(start, BLK)]
                    rhs[at + width : at + lanes, col : col + BLK] = jnp.zeros((lanes - width, BLK), BF16)
        for k in range(N_DP):
            first = pl.multiple_of((me ^ k) * rows, 16)
            outs[k][:, 2 * slot * BLK : (2 * slot + 2) * BLK] = jnp.dot(
                lhs[pl.ds(first, rows), :],
                rhs[:, 2 * slot * BLK : (2 * slot + 2) * BLK],
                preferred_element_type=F32,
            ).astype(BF16)


def lane_group(shape):
    return lax.broadcasted_iota(jnp.int32, shape, len(shape) - 1) // SUB


def activate_kernel(part0, part1, part2, part3, after, out, wide):
    rows = part0.shape[0]
    step = rows // N_XZ
    hidden = []
    for slot in range(SLOTS):
        total = part0[:, 2 * slot * BLK : (2 * slot + 2) * BLK].astype(F32)
        for part in (part1, part2, part3):
            total = total + part[:, 2 * slot * BLK : (2 * slot + 2) * BLK].astype(F32)
        gate, up = total[:, :BLK], total[:, BLK:]
        hidden.append(gate / (1.0 + jnp.exp(-gate)) * up)
    group = lane_group((rows, BLK))
    wide[rows:, :] = jnp.zeros((16, BLK), F32)
    for y in range(NY):
        mixed = jnp.zeros((rows, BLK), F32)
        for slot in range(SLOTS):
            shift = (slot - y) % NY * SUB
            rolled = pltpu.roll(hidden[slot], shift, 1) if shift else hidden[slot]
            mixed = jnp.where(group == slot, rolled, mixed)
        wide[:rows, :] = mixed
        for xz in range(N_XZ):
            out[xz * NY + y] = wide[step * xz : step * xz + 16, :].astype(BF16)


def arrange_kernel(where, source, got, after0, after1, out0, out1, out2, out3, send_own, quarters):
    me = where[1]
    group = lane_group((16, BLK))
    per_quarter = source.shape[0] // NY // N_DP
    for t in range(source.shape[0] // NY):
        mixed = jnp.zeros((16, BLK), F32)
        for b in range(NY):
            slot_id = source[t * NY + b]
            row = slot_id // SLOTS
            slot = slot_id - row * SLOTS
            shift = lax.rem((b - slot + NY) * SUB, BLK)
            rolled = pltpu.roll(got[row].astype(F32), shift, 1)
            mixed = jnp.where(group == b, rolled, mixed)
        mixed = mixed.astype(BF16)
        at = t % per_quarter * BLK
        quarters[t // per_quarter, :, at : at + BLK] = mixed
        send_own[2 * t] = mixed
        send_own[2 * t + 1] = mixed
    for k, out in enumerate((out0, out1, out2, out3)):
        out[...] = quarters[me ^ k]


def own_kernel(odd, got, out, wide):
    group = lane_group((16, BLK))
    step = out.shape[0] // N_XZ
    back = odd[0] * (2 * SUB)
    for xz in range(N_XZ):
        pieces = [got[xz * NY + y].astype(F32) for y in range(NY)]
        for blk in range(2):
            mixed = jnp.zeros((16, BLK), F32)
            for y in range(NY):
                shift = lax.rem(2 * BLK + (y - blk) * SUB - back, BLK)
                mixed = jnp.where(group == y, pltpu.roll(pieces[y], shift, 1), mixed)
            wide[xz * step : xz * step + 16, blk * BLK : (blk + 1) * BLK] = mixed
    out[...] = wide[: out.shape[0], :].astype(BF16)


def turn_kernel(own0, own1, own2, own3, out, parts, wide):
    step = own0.shape[0] // N_XZ
    for k, own in enumerate((own0, own1, own2, own3)):
        parts[k, : own.shape[0], :] = own[...].astype(F32)
        parts[k, own.shape[0] :, :] = jnp.zeros((16, own.shape[1]), F32)
    for xz in range(N_XZ):
        for k in range(N_DP):
            at = (xz * N_DP + k) * step
            wide[at : at + 16, :] = parts[k, xz * step : xz * step + 16, :]
    out[...] = wide[: out.shape[1], :].T.astype(BF16)


def cross_kernel(scaling, where, own0, own1, own2, own3, targets, out):
    rows = own0.shape[0]
    total = jnp.zeros(out.shape, F32)
    for k, own in enumerate((own0, own1, own2, own3)):
        first = pl.multiple_of((where[1] ^ k) * rows, 16)
        total += lax.dot_general(
            own[...], targets[pl.ds(first, rows), :], (((0,), (0,)), ((), ())), preferred_element_type=F32
        )
    out[...] = total * scaling


def gram_kernel(scaling, where, own, a_here, a_low, a_high, a_far0, a_far1, out, acc):
    y = where[0]
    half = a_far0.shape[0]

    def put(at, value):
        acc[at] = value

    put(y, jnp.dot(own[...], a_here[...], preferred_element_type=F32))
    put(lax.rem(y + 3, NY), jnp.dot(own[...], a_low[...], preferred_element_type=F32))
    put(lax.rem(y + 1, NY), jnp.dot(own[...], a_high[...], preferred_element_type=F32))
    put(
        lax.rem(y + 2, NY),
        jnp.dot(own[:, :half], a_far0[...], preferred_element_type=F32)
        + jnp.dot(own[:, half:], a_far1[...], preferred_element_type=F32),
    )
    group = lane_group((out.shape[0], BLK))
    for t in range(out.shape[1] // BLK // NY):
        parts = [acc[at, :, t * BLK : (t + 1) * BLK] * scaling for at in range(NY)]
        for b in range(NY):
            mixed = parts[b]
            for at in range(NY):
                if at != b:
                    mixed = jnp.where(group == at, pltpu.roll(parts[at], (at - b) % NY * SUB, 1), mixed)
            col = (t * NY + b) * BLK
            out[:, col : col + BLK] = mixed


def after_kernel(values, after, out):
    for i in range(values.shape[0]):
        for j in range(values.shape[1]):
            out[i, j] = values[i, j]


def copy_kernel(x, *refs):
    refs[-1][...] = x[...]


def after(values, *others):
    return pl.pallas_call(
        lambda got, *rest: after_kernel(got, rest[:-1], rest[-1]),
        out_shape=struct(values.shape, values.dtype),
        in_specs=[SMEM] + [ANY] * len(others),
        out_specs=SMEM,
    )(values, *others)


def pick_sources(dest_slot, block_count):
    slot_total = dest_slot.shape[0] * dest_slot.shape[1]
    slot_ids = jnp.arange(slot_total, dtype=jnp.int32)
    matches = dest_slot.reshape(-1)[None, :] == jnp.arange(block_count, dtype=jnp.int32)[:, None]
    return jnp.sum(jnp.where(matches, slot_ids[None, :], 0), axis=1)


def exchange(values):
    got = [values[0]]
    for k in range(1, N_DP):
        got.append(lax.ppermute(values[k], DP, [(i, i ^ k) for i in range(N_DP)]))
    return got


def swap_pairs():
    pairs = []
    for xh in range(2):
        for zh in range(2):
            for rest in range(16):
                for xl in range(2):
                    for c in range(2):
                        here = ((xh * 2 + zh) * 16 + rest) * 4 + xl * 2 + c
                        there = ((xl * 2 + c) * 16 + rest) * 4 + xh * 2 + zh
                        pairs.append((here, there))
    return pairs


def shift(x, axis, size, step):
    return lax.ppermute(x, axis, [(i, (i + step) % size) for i in range(size)])


def gather_copies(x, axis, size):
    copies = jnp.broadcast_to(x[None], (size, *x.shape))
    return lax.all_to_all(copies, axis, split_axis=0, concat_axis=0, tiled=True)


def ring(x, axis, size):
    found, low, high = [], x, x
    for step in range(1, size // 2):
        low, high = shift(low, axis, size, 1), shift(high, axis, size, -1)
        found += [(-step, low), (step, high)]
    half = x.shape[0] // 2
    far0 = shift(low[:half], axis, size, 1)
    far1 = shift(high[half:], axis, size, -1)
    return found, far0, far1


def local(tokens, targets, exp_gate, exp_up, exp_down, kept_block, dest_slot):
    rows = tokens.shape[0]
    quarter = exp_gate.shape[0]
    local_width = exp_gate.shape[1] // 2
    scaling = 1.0 / math.sqrt(rows * N_DP)
    xh, z, y = (lax.axis_index(name) for name in HID)
    where = jnp.stack([y, lax.axis_index(DP)]).astype(jnp.int32)
    source = pick_sources(dest_slot, 2 * N_HID)

    def both_halves(x):
        other = shift(x, "xh", XH, 1)
        return jnp.where(xh == 0, jnp.stack([x, other]), jnp.stack([other, x]))

    moved = lax.ppermute(tokens, HID + DP, swap_pairs())
    moved = jnp.pad(moved, ((0, 0), (0, BLK - moved.shape[1])))
    here = gather_copies(moved, ("xh", "z"), N_XZ)
    ((_, low), (_, high)), far0, far1 = ring(here, "y", NY)

    all_targets = both_halves(lax.all_gather(targets, "y", axis=0, tiled=True))
    all_targets = lax.all_gather(all_targets, "z", axis=0, tiled=False)
    all_targets = all_targets.transpose(1, 0, 2, 3).reshape(N_DP * rows, -1)

    chosen = after(kept_block, low, high)[0]
    down = exp_down.reshape(-1, N_HID, BLK // N_HID, quarter)[chosen]
    down = lax.all_to_all(down, HID, split_axis=1, concat_axis=0, tiled=True)

    parts = call(
        project_kernel,
        (struct((rows, 2 * SLOTS * BLK), BF16),) * N_DP,
        [SMEM, SMEM] + [VMEM] * 7,
        [pltpu.VMEM((N_DP * rows, 16 * BLK), BF16), pltpu.VMEM((16 * BLK, 2 * SLOTS * BLK), BF16)],
        where,
        kept_block,
        here,
        low,
        high,
        far0,
        far1,
        exp_gate,
        exp_up,
    )
    spread = call(
        activate_kernel,
        struct((N_HID, 16, BLK), BF16),
        [VMEM] * N_DP + [ANY],
        [pltpu.VMEM((rows + 16, BLK), F32)],
        *exchange(parts),
        down,
    )
    spread = lax.all_to_all(spread, HID, split_axis=0, concat_axis=0, tiled=True)
    down = down.reshape(N_HID * SLOTS, BLK // N_HID, quarter).at[source].get(mode="promise_in_bounds")
    *quarters, send_own = call(
        arrange_kernel,
        (struct((16, 1024), BF16),) * N_DP + (struct((N_HID, 16, BLK), BF16),),
        [SMEM, SMEM, VMEM, ANY, ANY],
        [pltpu.VMEM((N_DP, 16, 1024), BF16)],
        where,
        source,
        spread,
        all_targets,
        down,
    )
    step = rows // N_XZ
    mine = jnp.concatenate([x[:step] for x in exchange(quarters)], axis=0)

    a_here = gather_copies(mine, ("xh", "z"), N_XZ).reshape(N_DP * rows, -1)
    ((_, a_low), (_, a_high)), a_far0, a_far1 = ring(a_here, "y", NY)

    send_own = call(copy_kernel, struct(send_own.shape, BF16), [VMEM, ANY], [], send_own, a_here)
    got_own = lax.all_to_all(send_own, HID, split_axis=0, concat_axis=0, tiled=True)
    own = call(
        own_kernel,
        struct((rows, local_width), BF16),
        [SMEM, VMEM],
        [pltpu.VMEM((rows + 16, local_width), F32)],
        lax.rem(y, 2).reshape(1),
        got_own,
    )
    own = exchange([own] * N_DP)
    own_turned = call(
        turn_kernel,
        struct((local_width, N_DP * rows), BF16),
        [VMEM] * N_DP,
        [pltpu.VMEM((N_DP, rows + 16, local_width), F32), pltpu.VMEM((N_DP * rows + 16, local_width), F32)],
        *own,
    )
    cross_prod = call(
        lambda *refs: cross_kernel(scaling, *refs),
        struct((local_width, quarter), F32),
        [SMEM] + [VMEM] * 5,
        [],
        where,
        *own,
        all_targets,
    )
    gram_sum = call(
        lambda *refs: gram_kernel(scaling, *refs),
        struct((local_width, N_HID // N_DP * local_width), F32),
        [SMEM] + [VMEM] * 6,
        [pltpu.VMEM((NY, local_width, 1024), F32)],
        where,
        own_turned,
        a_here,
        a_low,
        a_high,
        a_far0,
        a_far1,
    )

    down = call(copy_kernel, struct(down.shape, BF16), [VMEM] + [ANY] * 3, [], down, got_own, a_low, a_high)
    down = lax.all_to_all(down.reshape(N_HID, 2, BLK // N_HID, quarter), HID, split_axis=0, concat_axis=0, tiled=True)
    dense_down = down.transpose(1, 0, 2, 3).reshape(local_width, quarter)
    return (gram_sum, cross_prod, dense_down)


def solution(mesh):
    fine = Mesh(mesh.devices.reshape(XH, NZ, NY, XL, NC), HID + DP)
    return jax.shard_map(
        local,
        mesh=fine,
        in_specs=(P(DP, HID), P(HID, DP), P(DP, HID), P(DP, HID), P(HID, DP), P(HID, None), P()),
        out_specs=(P(HID, DP), P(HID, DP), P(HID, DP)),
        check_vma=False,
    )
```
